32 devices in a mesh: groups: 2 (over y), space: 8 (over z, x), tm: 2 (over core).
Axes of the slice: x: 2, y: 2, z: 4, core: 2. Of those that a mesh axis runs over, the one named last changes fastest.
Arguments:
- probes: float32 [16, 4096, 128], P(('groups', 'tm'), 'space'), parts along dimension 0, may hold values from -60 to 60
- phi: float32 [16, 4096], P(('groups', 'tm'), 'space'), parts along dimension 0, may hold values from -0.4 to 0.4
- kcols: int32 [32, 3], P('space'), may hold values from 0 to 31, as said below
- kblocks: float32 [32, 3, 128, 128], P('space'), may hold values from -0.25 to 0.85
Outputs:
- solution: float32 [16, 4096, 128], P(('groups', 'tm'), 'space'), parts along dimension 0
- residual: float32 [16, 4096, 128], P(('groups', 'tm'), 'space'), parts along dimension 0
The draws below stay inside these ranges and needn't reach their ends.
There are 2 independent parts, one for each index of `groups`. The reference program is written for one: setup_inputs(seed, part) draws one part's arguments, and reference() takes and returns one part's arrays. A program takes and returns all parts, laid end to end along the dimension named above; an argument that names none is the same for every part. Nothing has to cross between parts.
Inputs may be any that keep to these rules, and one draw needn't show every extreme that they name: `kcols`: block row i lists block i first, then two distinct other blocks, each within 2 blocks of i.
All inputs are finite; a program needn't handle non-finite values.
Results may differ from the reference program's by a relative error of at most 0.00013.
Values sent between devices are 32-bit elements; how exact they have to be, the bound alone decides.
A program may use at most 64 MiB of HBM per device.

```python
import math
import jax
import jax.numpy as jnp
from jax import lax

BLOCK = 128
PROBES = 128
ITERS = 2
NNZ = 3
REACH = 2
NB = 32
NS = 4096
L = 8


def draw_kcols(key, part):
    key = jax.random.fold_in(key, 11)
    key_near, key_step, key_sign = jax.random.split(key, 3)
    block_rows = jnp.arange(NB, dtype=jnp.int32)
    near_step = jax.random.randint(key_near, (NB,), 1, REACH + 1)
    shift_step = jax.random.randint(key_step, (NB,), 1, REACH)
    far_step = (near_step - 1 + shift_step) % REACH + 1
    sign_pick = jax.random.randint(key_sign, (NB, 2), 0, 2) * 2 - 1

    def reflect(offset):
        ahead = block_rows + offset
        inside = (ahead >= 0) & (ahead < NB)
        return jnp.where(inside, ahead, block_rows - offset)
    result = jnp.stack([block_rows, reflect(sign_pick[:, 0] * near_step), reflect(sign_pick[:, 1] * far_step)], axis=1)
    return result.astype(jnp.int32)


def draw_kblocks(key, part):
    key = jax.random.fold_in(key, 12)
    dims_all = (NB, NNZ, BLOCK, BLOCK)
    spread_scale = 0.35 / math.sqrt(3.0 * BLOCK)
    values = jnp.clip(jax.random.normal(key, dims_all, jnp.float32), -4.0, 4.0) * spread_scale
    row_index = lax.broadcasted_iota(jnp.int32, dims_all, 2)
    col_index = lax.broadcasted_iota(jnp.int32, dims_all, 3)
    slot_index = lax.broadcasted_iota(jnp.int32, dims_all, 1)
    diagonal_mark = ((row_index == col_index) & (slot_index == 0)).astype(jnp.float32)
    return values + 0.6 * diagonal_mark


def draw_probes(key, part):
    key = jax.random.fold_in(key, 13)
    key_vals, key_cols = jax.random.split(key, 2)
    dims_all = (L, NS, PROBES)
    site_pos = jnp.arange(NS, dtype=jnp.float32) / NS
    col_scale = 10.0 ** (jax.random.uniform(key_cols, (PROBES,), jnp.float32) - 0.5)
    values = jnp.clip(jax.random.normal(key_vals, dims_all, jnp.float32), -4.0, 4.0)
    growth = math.log(3.0)
    return values * jnp.exp(growth * site_pos)[None, :, None] * col_scale[None, None, :]


def shard_levels(rng, extent, shards, least, high):
    factor_of, own = 1.0, jax.random.fold_in(rng, 6)
    for position, parts in shards:
        heights = jnp.exp(jax.random.uniform(jax.random.fold_in(own, position), (parts,), jnp.float32, least / len(shards), high / len(shards)))
        factor_of = factor_of * jnp.repeat(heights, extent[position] // parts).reshape([-1 if axis == position else 1 for axis in range(len(extent))])
    return factor_of


def setup_inputs(seed: int = 0, part: int = 0) -> dict:
    streams_of = jax.random.split(jax.random.key(seed), 5)
    part_splits = jax.random.split(jax.random.fold_in(streams_of[4], part), 5)
    return {
        "probes": draw_probes(jax.random.fold_in(jax.random.fold_in(streams_of[4], part), 71), part),
        "phi": jnp.clip(jax.random.uniform(part_splits[1], (L, NS), jnp.float32, -0.4, 0.4) * shard_levels(part_splits[1], (L, NS), ((0, 2), (1, 8)), -0.4, 0.0), -0.4, 0.4),
        "kcols": draw_kcols(jax.random.fold_in(streams_of[4], 71), part),
        "kblocks": draw_kblocks(jax.random.fold_in(streams_of[4], 71), part),
    }


def hop_apply(panel, kcols, kblocks):
    block_size = kblocks.shape[2]
    pieces = panel.reshape(kblocks.shape[0], block_size, panel.shape[-1])
    picked = pieces[kcols]
    result = jnp.einsum('nkab,nkbp->nap', kblocks, picked, precision=lax.Precision.HIGHEST)
    return result.reshape(panel.shape)


def hop_transpose(panel, kcols, kblocks):
    block_size = kblocks.shape[2]
    pieces = panel.reshape(kblocks.shape[0], block_size, panel.shape[-1])
    terms = jnp.einsum('nkba,nbp->nkap', kblocks, pieces, precision=lax.Precision.HIGHEST)
    summed = jnp.zeros_like(pieces).at[kcols.reshape(-1)].add(terms.reshape(-1, block_size, panel.shape[-1]))
    return summed.reshape(panel.shape)


def apply_forward(vector, field, kcols, kblocks):
    earlier = jnp.concatenate([-vector[-1:], vector[:-1]], axis=0)
    scaled = field[:, :, None] * earlier
    moved = lax.map(lambda panel: hop_apply(panel, kcols, kblocks), scaled)
    return vector - moved


def apply_backward(vector, field, kcols, kblocks):
    moved = lax.map(lambda panel: hop_transpose(panel, kcols, kblocks), vector)
    scaled = field[:, :, None] * moved
    later = jnp.concatenate([scaled[1:], -scaled[:1]], axis=0)
    return vector - later


def reference(probes, phi, kcols, kblocks):
    field = jnp.exp(phi)
    solution = jnp.zeros_like(probes)
    residual = probes
    direction = probes
    norm_now = jnp.sum(residual * residual, axis=(0, 1))
    for iteration in range(ITERS):
        image = apply_forward(direction, field, kcols, kblocks)
        alpha = norm_now / jnp.sum(image * image, axis=(0, 1))
        solution = solution + alpha * direction
        residual = residual - alpha * apply_backward(image, field, kcols, kblocks)
        norm_next = jnp.sum(residual * residual, axis=(0, 1))
        direction = residual + (norm_next / norm_now) * direction
        norm_now = norm_next
    return solution, residual
```

```python
import functools

import jax
import jax.numpy as jnp
from jax import lax
from jax.experimental import pallas as pl
from jax.experimental.pallas import tpu as pltpu
from jax.sharding import PartitionSpec as P

MESH = pl.DeviceIdType.MESH
B = 128
OFFS = (-2, -1, 1, 2)


PX, SMALL, KX, KC, TM, DOWN, UP, R1X, R2X, CX = 0, 1, 2, 3, 4, 8, 12, 16, 17, 18
NSEM = 19


def roll64(x):
    return pltpu.roll(x, 64, axis=1)


def split(x):
    high = x.astype(jnp.bfloat16)
    return high, (x - high.astype(jnp.float32)).astype(jnp.bfloat16)


def dot(a, b):
    return jnp.dot(a, b, preferred_element_type=jnp.float32)


def kernel(
    pairs, x_ref, small_ref, k_ref, sol_ref, res_ref,
    px, d, f, sc1, sc2, im, y, r1, r2, r1p, r2p, yr, tms, tmr, smalls, kraw,
    kh, kl, kth, ktl, vh, vl, redsrc, red, coef, coefp,
    ssem, rsem, redss, redrs, lsem,
):
    g, s, t = lax.axis_index("groups"), lax.axis_index("space"), lax.axis_index("tm")
    p, h = s // 2, s % 2
    o = 1 - h
    team = 2 * pairs
    me = p * 2 + t
    peer = (g, s + 1 - 2 * h, t)
    mate = (g, s, 1 - t)
    below = (g, jnp.maximum(s - 2, 0), t)
    above = (g, jnp.minimum(s + 2, 2 * pairs - 1), t)
    has_below, has_above = p > 0, p < pairs - 1

    def member(index):
        return (g, (index // 2) * 2 + h, index % 2)

    barrier = pltpu.get_barrier_semaphore()

    @pl.loop(0, team - 1)
    def _(i):
        pl.semaphore_signal(
            barrier, inc=1, device_id=member(lax.rem(me + 1 + i, team)), device_id_type=MESH
        )

    pl.semaphore_signal(barrier, inc=1, device_id=peer, device_id_type=MESH)

    lane = lax.broadcasted_iota(jnp.int32, (1, 128), 1)
    left = lane < 64
    is0 = h == 0

    def remote(src, dst, index, device):
        return pltpu.make_async_remote_copy(
            src_ref=src, dst_ref=dst, send_sem=ssem.at[index], recv_sem=rsem.at[index],
            device_id=device, device_id_type=MESH,
        )

    own_rows = pl.ds(pl.multiple_of(h * 512, 512), 512)
    peer_rows = pl.ds(pl.multiple_of(o * 512, 512), 512)
    kown = pltpu.make_async_copy(k_ref, kraw.at[pl.ds(h * 12, 12)], lsem)
    kown.start()

    @pl.loop(0, 4)
    def _(i):
        rows = pl.ds(pl.multiple_of(i * B, B), B)
        mine_rows = pl.ds(pl.multiple_of(h * 512 + i * B, B), B)
        for a in range(2):
            xa, xb = x_ref[a, rows, :], x_ref[a + 2, rows, :]
            low = jnp.where(left, xa, roll64(xb))
            high = jnp.where(left, roll64(xa), xb)
            cols = slice(a * 128, a * 128 + 128)
            px[rows, cols] = jnp.where(is0, high, low)
            d[mine_rows, cols] = jnp.where(is0, low, high)

    smalls[h] = small_ref[...]
    pl.semaphore_wait(barrier, team)

    c_px = remote(px, d.at[own_rows], PX, peer)
    c_px.start()
    c_small = remote(small_ref, smalls.at[h], SMALL, peer)
    c_small.start()
    c_kx = remote(k_ref.at[pl.ds(t * 6, 6)], kraw.at[pl.ds(h * 12 + t * 6, 6)], KX, peer)
    c_kx.start()

    def make_field(half):
        @pl.loop(0, 4)
        def _(j):
            e = jnp.exp(smalls[half, pl.ds(pl.multiple_of(j * 16 + 8, 8), 8), :])
            rows = pl.ds(pl.multiple_of(half * 512 + j * B, B), B)
            top = lax.broadcasted_iota(jnp.int32, (B, 128), 0) < 64
            for a in range(2):
                m = jnp.where(top, e[a : a + 1, :], e[a + 2 : a + 3, :])
                f[rows, a * 128 : a * 128 + 128] = m.T

    def make_bands(half):
        @pl.loop(0, 2)
        def _(jj):
            band = half * 2 + jj
            for ri in range(2):
                j = jj * 2 + ri
                k0, k1, k2 = (kraw[half * 12 + 3 * j + k] for k in range(3))
                t0, t1, t2 = k0.T, k1.T, k2.T
                sel = smalls[half, pl.ds(pl.multiple_of(j * 16, 8), 8), :]
                rr = slice(ri * B, ri * B + B)
                empty = 5 * (1 - ri)
                ec = slice(empty * B, empty * B + B)
                zero = jnp.zeros((B, B), jnp.bfloat16)
                kh[band, rr, ec] = zero
                kl[band, rr, ec] = zero
                kth[band, ec, rr] = zero
                ktl[band, ec, rr] = zero
                for off in range(-2, 3):
                    w = off + 2 + ri
                    wc = slice(w * B, w * B + B)
                    if off == 0:
                        blk, blt = k0, t0
                    else:
                        i1 = OFFS.index(off)
                        s1, s2 = sel[i1 : i1 + 1, :], sel[4 + i1 : 5 + i1, :]
                        blk, blt = s1 * k1 + s2 * k2, s1 * t1 + s2 * t2
                    kh[band, rr, wc], kl[band, rr, wc] = split(blk)
                    kth[band, wc, rr], ktl[band, wc, rr] = split(blt)

    def swap_slices(panel, cols, n, first_half_rolled):
        a, b = panel[0:512, cols], panel[512:1024, cols]
        if first_half_rolled:
            tms[n] = jnp.where(left, roll64(a), b)
        else:
            tms[n] = jnp.where(left, a, roll64(b))
        copy = remote(tms.at[n], tmr.at[n], TM + n, mate)
        copy.start()
        return copy

    def halo(low_src, low_dst, high_src, high_dst, n):
        down = remote(low_src, low_dst, DOWN + n, below)
        up = remote(high_src, high_dst, UP + n, above)

        @pl.when(has_below)
        def _():
            down.start()

        @pl.when(has_above)
        def _():
            up.start()

        return down, up

    def halo_arrived(copies):
        down, up = copies

        @pl.when(has_above)
        def _():
            down.wait_recv()

        @pl.when(has_below)
        def _():
            up.wait_recv()

    def halo_sent(copies):
        down, up = copies

        @pl.when(has_below)
        def _():
            down.wait_send()

        @pl.when(has_above)
        def _():
            up.wait_send()

    def scaled_earlier(panel, out, n, copy):
        copy.wait_recv()
        sign = jnp.where(t == 0, -1.0, 1.0)
        got = tmr[n]
        rolled = roll64(panel[:, 128:256])
        out[256:768, 0:128] = f[0:512, 0:128] * jnp.where(left, sign * got, rolled[0:512])
        out[768:1280, 0:128] = f[512:1024, 0:128] * jnp.where(
            left, sign * roll64(got), rolled[512:1024]
        )
        out[256:1280, 128:256] = f[:, 128:256] * panel[:, 0:128]

    def squares(panel):
        q = panel[...]
        q = jnp.sum((q * q).reshape(128, 8, 256), axis=0)
        q = q[:, 0:128] + q[:, 128:256]
        return q + roll64(q)

    def reduce_start(n):
        @pl.loop(0, team - 1)
        def _(i):
            pltpu.make_async_remote_copy(
                src_ref=redsrc.at[n], dst_ref=red.at[n, team - 2 - i],
                send_sem=redss.at[n], recv_sem=redrs.at[n],
                device_id=member(lax.rem(me + 1 + i, team)), device_id_type=MESH,
            ).start()

    def reduce_done(n):
        pltpu.make_async_copy(red.at[n], red.at[n], redrs.at[n]).wait()
        total = redsrc[n] + jnp.sum(red[n], axis=0)
        return (
            jnp.sum(total[0:8], axis=0, keepdims=True),
            jnp.sum(total[8:16], axis=0, keepdims=True),
        )

    def twice(v):
        return jnp.concatenate([v, v], axis=1)

    def forward():
        @pl.loop(0, 4)
        def _(i):
            win = pl.ds(pl.multiple_of(i * 256, 256), 768)
            rows = pl.ds(pl.multiple_of(i * 256, 256), 256)
            vhi = vh[win, :]
            acc = dot(kh[i], vhi) + dot(kl[i], vhi) + dot(kh[i], vl[win, :])
            im[rows, :] = d[rows, :] - acc

    def back_part(i):
        zh, zl = split(im[pl.ds(pl.multiple_of(i * 256, 256), 256), :])
        return dot(kth[i], zh) + dot(ktl[i], zh) + dot(kth[i], zl)

    def backward(n):
        @pl.loop(0, 2)
        def _(i):
            y[pl.ds(pl.multiple_of(i * 768, 256), 768), :] = back_part(i * 3)

        copies = halo(
            y.at[0:256], yr.at[n, 1], y.at[1280:1536], yr.at[n, 0], 1 + 2 * n
        )

        @pl.loop(1, 3)
        def _(i):
            win = pl.ds(pl.multiple_of(i * 256, 256), 768)
            y[win, :] += back_part(i)

        return copies

    def apply_later(n, copies, source, out, alpha):
        halo_arrived(copies)
        y[256:512, :] = f[0:256, :] * (y[256:512, :] + yr[n, 0])
        y[512:1024, :] = f[256:768, :] * y[512:1024, :]
        y[1024:1280, :] = f[768:1024, :] * (y[1024:1280, :] + yr[n, 1])
        slot = 1 + 2 * n
        copy = swap_slices(y.at[256:1280], slice(0, 128), slot, False)
        a1 = alpha
        out[:, 0:128] = source[:, 0:128] - a1 * (im[:, 0:128] - y[256:1280, 128:256])
        copy.wait_recv()
        sign = jnp.where(t == 1, -1.0, 1.0)
        got = tmr[slot]
        rolled = roll64(y[256:1280, 0:128])
        out[0:512, 128:256] = source[0:512, 128:256] - a1 * (
            im[0:512, 128:256] - jnp.where(left, rolled[0:512], sign * roll64(got))
        )
        out[512:1024, 128:256] = source[512:1024, 128:256] - a1 * (
            im[512:1024, 128:256] - jnp.where(left, rolled[512:1024], sign * got)
        )
        return copy

    @pl.when(jnp.logical_not(has_below))
    def _():
        for ref in (sc1, sc2):
            ref[0:256, :] = jnp.zeros((256, 256), jnp.float32)
        for n in range(2):
            yr[n, 0] = jnp.zeros((256, 256), jnp.float32)

    @pl.when(jnp.logical_not(has_above))
    def _():
        for ref in (sc1, sc2):
            ref[1280:1536, :] = jnp.zeros((256, 256), jnp.float32)
        for n in range(2):
            yr[n, 1] = jnp.zeros((256, 256), jnp.float32)

    make_field(h)
    kown.wait()
    make_bands(h)
    c_px.wait_recv()
    t0 = swap_slices(d, slice(128, 256), 0, True)
    c_small.wait_recv()
    make_field(o)
    scaled_earlier(d, sc1, 0, t0)
    h0 = halo(sc1.at[256:512], sc1.at[1280:1536], sc1.at[1024:1280], sc1.at[0:256], 0)
    redsrc[0, 0:8] = squares(d)
    c_kx.wait_recv()
    got_k = kraw.at[pl.ds(o * 12 + t * 6, 6)]
    c_kc = remote(got_k, got_k, KC, mate)
    c_kc.start()
    c_kc.wait_recv()
    make_bands(o)
    halo_arrived(h0)
    vh[...], vl[...] = split(sc1[...])
    forward()
    redsrc[0, 8:16] = squares(im)
    reduce_start(0)
    b0 = backward(0)
    rr0, im_sum = reduce_done(0)
    alpha1 = rr0 / im_sum
    t1 = apply_later(0, b0, d, r1, alpha1)
    c_r1 = remote(r1.at[peer_rows], r1p, R1X, peer)
    t2 = swap_slices(r1, slice(128, 256), 2, True)
    redsrc[1, 0:8] = squares(r1)
    redsrc[1, 8:16] = jnp.zeros((8, 128), jnp.float32)
    reduce_start(1)
    scaled_earlier(r1, sc2, 2, t2)
    h1 = halo(sc2.at[256:512], sc2.at[1280:1536], sc2.at[1024:1280], sc2.at[0:256], 2)
    c_r1.start()

    rr1, _ = reduce_done(1)
    beta = rr1 / rr0
    beta2 = twice(beta)
    d[...] = r1[...] + beta2 * d[...]
    halo_arrived(h1)
    vh[...], vl[...] = split(sc2[...] + beta2 * sc1[...])
    forward()
    redsrc[2, 0:8] = squares(im)
    redsrc[2, 8:16] = jnp.zeros((8, 128), jnp.float32)
    reduce_start(2)
    halo_sent(b0)
    b1 = backward(1)
    im_sum, _ = reduce_done(2)
    alpha2 = rr1 / im_sum
    coef[0:8, :] = jnp.broadcast_to(alpha1 + alpha2 * beta, (8, 128))
    coef[8:16, :] = jnp.broadcast_to(alpha2, (8, 128))
    c_cx = remote(coef, coefp, CX, peer)
    c_cx.start()
    t3 = apply_later(1, b1, r1, r2, alpha2)
    c_r2 = remote(r2.at[peer_rows], r2p, R2X, peer)
    c_r2.start()

    def unpack(own, other):
        low = jnp.where(is0, own, other)
        high = jnp.where(is0, other, own)
        return jnp.where(left, low, roll64(high)), jnp.where(left, roll64(low), high)

    c_cx.wait_recv()
    c_r1.wait_recv()
    low_coef = jnp.where(is0, coef[...], coefp[...])
    high_coef = jnp.where(is0, coefp[...], coef[...])
    full = jnp.where(left, low_coef, high_coef)
    cp, cr = full[0:1], full[8:9]

    @pl.loop(0, 4)
    def _(i):
        rows = pl.ds(pl.multiple_of(i * B, B), B)
        mine_rows = pl.ds(pl.multiple_of(h * 512 + i * B, B), B)
        for a in range(2):
            cols = slice(a * 128, a * 128 + 128)
            va, vb = unpack(r1[mine_rows, cols], r1p[rows, cols])
            sol_ref[a, rows, :] = cp * x_ref[a, rows, :] + cr * va
            sol_ref[a + 2, rows, :] = cp * x_ref[a + 2, rows, :] + cr * vb

    c_r2.wait_recv()

    @pl.loop(0, 4)
    def _(i):
        rows = pl.ds(pl.multiple_of(i * B, B), B)
        mine_rows = pl.ds(pl.multiple_of(h * 512 + i * B, B), B)
        for a in range(2):
            cols = slice(a * 128, a * 128 + 128)
            va, vb = unpack(r2[mine_rows, cols], r2p[rows, cols])
            res_ref[a, rows, :] = va
            res_ref[a + 2, rows, :] = vb

    for copy in (c_px, c_small, c_kx, c_kc, t0, t1, t2, t3, c_r1, c_cx, c_r2):
        copy.wait_send()
    for copies in (h0, h1, b1):
        halo_sent(copies)
    for n in range(3):
        pltpu.make_async_copy(red.at[n], red.at[n], redss.at[n]).wait()


def local(probes, phi, kcols, kblocks):
    pairs = lax.axis_size("space") // 2
    own = kcols.shape[0]
    first = lax.axis_index("space") * own
    offset = kcols - (first + jnp.arange(own, dtype=jnp.int32))[:, None]
    chosen = offset[:, 1:, None] == jnp.array(OFFS, jnp.int32)[None, None, :]
    chosen = chosen.astype(jnp.float32).reshape(own, 8)
    chosen = jnp.broadcast_to(chosen[:, :, None], (own, 8, 128))
    angles = phi.reshape(4, own, B).transpose(1, 0, 2)
    angles = jnp.concatenate([angles, jnp.zeros_like(angles)], axis=1)
    small = jnp.concatenate([chosen, angles], axis=1).reshape(own * 16, 128)
    f32, bf16 = jnp.float32, jnp.bfloat16
    vmem = pl.BlockSpec(memory_space=pltpu.VMEM)
    team = 2 * pairs
    return pl.pallas_call(
        functools.partial(kernel, pairs),
        out_shape=[jax.ShapeDtypeStruct(probes.shape, f32)] * 2,
        in_specs=[vmem, vmem, pl.BlockSpec(memory_space=pl.ANY)],
        out_specs=[vmem, vmem],
        scratch_shapes=[
            pltpu.VMEM((512, 256), f32),
            pltpu.VMEM((1024, 256), f32),
            pltpu.VMEM((1024, 256), f32),
            pltpu.VMEM((1536, 256), f32),
            pltpu.VMEM((1536, 256), f32),
            pltpu.VMEM((1024, 256), f32),
            pltpu.VMEM((1536, 256), f32),
            pltpu.VMEM((1024, 256), f32),
            pltpu.VMEM((1024, 256), f32),
            pltpu.VMEM((512, 256), f32),
            pltpu.VMEM((512, 256), f32),
            pltpu.VMEM((2, 2, 256, 256), f32),
            pltpu.VMEM((4, 512, 128), f32),
            pltpu.VMEM((4, 512, 128), f32),
            pltpu.VMEM((2, 64, 128), f32),
            pltpu.VMEM((24, 128, 128), f32),
            pltpu.VMEM((4, 256, 768), bf16),
            pltpu.VMEM((4, 256, 768), bf16),
            pltpu.VMEM((4, 768, 256), bf16),
            pltpu.VMEM((4, 768, 256), bf16),
            pltpu.VMEM((1536, 256), bf16),
            pltpu.VMEM((1536, 256), bf16),
            pltpu.VMEM((3, 16, 128), f32),
            pltpu.VMEM((3, team - 1, 16, 128), f32),
            pltpu.VMEM((16, 128), f32),
            pltpu.VMEM((16, 128), f32),
            pltpu.SemaphoreType.DMA((NSEM,)),
            pltpu.SemaphoreType.DMA((NSEM,)),
            pltpu.SemaphoreType.DMA((3,)),
            pltpu.SemaphoreType.DMA((3,)),
            pltpu.SemaphoreType.DMA,
        ],
        compiler_params=pltpu.CompilerParams(
            collective_id=0, has_side_effects=True, vmem_limit_bytes=50 * 1024 * 1024
        ),
    )(probes, small, kblocks.reshape(own * 3, B, B))


def solution(mesh):
    panel = P(("groups", "tm"), "space", None)
    return jax.shard_map(
        local,
        mesh=mesh,
        in_specs=(
            panel, P(("groups", "tm"), "space"), P("space", None), P("space", None, None, None),
        ),
        out_specs=(panel, panel),
        check_vma=False,
    )
```

```python
import functools

import jax
import jax.numpy as jnp
from jax import lax
from jax.experimental import pallas as pl
from jax.experimental.pallas import tpu as pltpu
from jax.sharding import PartitionSpec as P

MESH = pl.DeviceIdType.MESH
B = 128
OFFS = (-2, -1, 1, 2)


SMALL, KX, KY, KC, KD, R1X, CX, PX, R2X, DOWN, UP, TM = 0, 1, 2, 3, 4, 5, 6, 7, 9, 11, 15, 19
NSEM = 27

RIM, INNER = 0, 1
RUNS = (((0, 256), (768, 1024)), ((256, 512), (512, 768)))


def roll64(x):
    return pltpu.roll(x, 64, axis=1)


def split(x):
    high = x.astype(jnp.bfloat16)
    return high, (x - high.astype(jnp.float32)).astype(jnp.bfloat16)


def dot(a, b):
    return jnp.dot(a, b, preferred_element_type=jnp.float32)


def kernel(
    pairs, x_hbm, phi_ref, cols_ref, k_ref, sol_ref, res_ref,
    x_ref, px, d, f, sc1, sc2, im, y, r1, r2, r1p, r2p, yr, tms, tmr, smalls, kraw,
    kh, kl, kth, ktl, vh, vl, redsrc, red, coef, coefp,
    ssem, rsem, redss, redrs, lsem, xsem,
):
    g, s, t = lax.axis_index("groups"), lax.axis_index("space"), lax.axis_index("tm")
    p, h = s // 2, s % 2
    o = 1 - h
    team = 2 * pairs
    me = p * 2 + t
    peer = (g, s + 1 - 2 * h, t)
    mate = (g, s, 1 - t)
    twin = (1 - g, s, t)
    below = (g, jnp.maximum(s - 2, 0), t)
    above = (g, jnp.minimum(s + 2, 2 * pairs - 1), t)
    has_below, has_above = p > 0, p < pairs - 1

    def member(index):
        return (g, (index // 2) * 2 + h, index % 2)

    barrier = pltpu.get_barrier_semaphore()

    @pl.loop(0, team - 1)
    def _(i):
        pl.semaphore_signal(
            barrier, inc=1, device_id=member(lax.rem(me + 1 + i, team)), device_id_type=MESH
        )

    pl.semaphore_signal(barrier, inc=1, device_id=peer, device_id_type=MESH)
    pl.semaphore_signal(barrier, inc=1, device_id=twin, device_id_type=MESH)
    xload = pltpu.make_async_copy(x_hbm, x_ref, xsem)
    xload.start()

    lane = lax.broadcasted_iota(jnp.int32, (1, 128), 1)
    left = lane < 64
    is0 = h == 0

    def remote(src, dst, index, device):
        return pltpu.make_async_remote_copy(
            src_ref=src, dst_ref=dst, send_sem=ssem.at[index], recv_sem=rsem.at[index],
            device_id=device, device_id_type=MESH,
        )

    peer_rows = pl.ds(pl.multiple_of(o * 512, 512), 512)
    part_rows = (
        pl.ds(pl.multiple_of(o * 768, 256), 256),
        pl.ds(pl.multiple_of(256 + o * 256, 256), 256),
    )
    part_at = (
        pl.ds(pl.multiple_of(o * 256, 256), 256),
        pl.ds(pl.multiple_of(h * 256, 256), 256),
    )
    own_part_rows = (
        pl.ds(pl.multiple_of(h * 768, 256), 256),
        pl.ds(pl.multiple_of(256 + h * 256, 256), 256),
    )
    own_part_at = (
        pl.ds(pl.multiple_of(h * 256, 256), 256),
        pl.ds(pl.multiple_of(o * 256, 256), 256),
    )
    kown = pltpu.make_async_copy(k_ref, kraw.at[pl.ds(h * 12, 12)], lsem)
    kown.start()

    sub = lax.broadcasted_iota(jnp.int32, (8, 128), 0)
    for j in range(4):
        chosen = jnp.zeros((8, 128), jnp.float32)
        for k in range(2):
            distance = cols_ref[j, 1 + k] - (s * 4 + j)
            for i1, off in enumerate(OFFS):
                hit = jnp.where(distance == off, 1.0, 0.0)
                chosen = jnp.where(sub == 4 * k + i1, hit, chosen)
        smalls[h, j * 16 : j * 16 + 8, :] = chosen
        part = phi_ref[:, j * B : j * B + B]
        smalls[h, j * 16 + 8 : j * 16 + 16, :] = jnp.concatenate([part, part], axis=0)

    xload.wait()

    @pl.loop(0, 4)
    def _(i):
        rows = pl.ds(pl.multiple_of(i * B, B), B)
        mine_rows = pl.ds(pl.multiple_of(h * 512 + i * B, B), B)
        for a in range(2):
            xa, xb = x_ref[a, rows, :], x_ref[a + 2, rows, :]
            low = jnp.where(left, xa, roll64(xb))
            high = jnp.where(left, roll64(xa), xb)
            cols = slice(a * 128, a * 128 + 128)
            px[rows, cols] = jnp.where(is0, high, low)
            d[mine_rows, cols] = jnp.where(is0, low, high)

    pl.semaphore_wait(barrier, team + 1)

    c_small = remote(smalls.at[h], smalls.at[h], SMALL, peer)
    c_small.start()
    c_px = [
        remote(px.at[own_part_at[n]], d.at[own_part_rows[n]], PX + n, peer) for n in range(2)
    ]
    c_px[RIM].start()
    row = g * 2 + t
    sent_k = pl.ds(h * 12 + row * 3, 3)
    c_kx = remote(k_ref.at[pl.ds(row * 3, 3)], kraw.at[sent_k], KX, peer)
    c_kx.start()
    c_px[INNER].start()

    def make_field(half):
        @pl.loop(0, 4)
        def _(j):
            e = jnp.exp(smalls[half, pl.ds(pl.multiple_of(j * 16 + 8, 8), 8), :])
            rows = pl.ds(pl.multiple_of(half * 512 + j * B, B), B)
            top = lax.broadcasted_iota(jnp.int32, (B, 128), 0) < 64
            for a in range(2):
                m = jnp.where(top, e[a : a + 1, :], e[a + 2 : a + 3, :])
                f[rows, a * 128 : a * 128 + 128] = m.T

    def make_bands(half):
        @pl.loop(0, 2)
        def _(jj):
            band = half * 2 + jj
            for ri in range(2):
                j = jj * 2 + ri
                k0, k1, k2 = (kraw[half * 12 + 3 * j + k] for k in range(3))
                t0, t1, t2 = k0.T, k1.T, k2.T
                sel = smalls[half, pl.ds(pl.multiple_of(j * 16, 8), 8), :]
                rr = slice(ri * B, ri * B + B)
                empty = 5 * (1 - ri)
                ec = slice(empty * B, empty * B + B)
                zero = jnp.zeros((B, B), jnp.bfloat16)
                kh[band, rr, ec] = zero
                kl[band, rr, ec] = zero
                kth[band, ec, rr] = zero
                ktl[band, ec, rr] = zero
                for off in range(-2, 3):
                    w = off + 2 + ri
                    wc = slice(w * B, w * B + B)
                    if off == 0:
                        blk, blt = k0, t0
                    else:
                        i1 = OFFS.index(off)
                        s1, s2 = sel[i1 : i1 + 1, :], sel[4 + i1 : 5 + i1, :]
                        blk, blt = s1 * k1 + s2 * k2, s1 * t1 + s2 * t2
                    kh[band, rr, wc], kl[band, rr, wc] = split(blk)
                    kth[band, wc, rr], ktl[band, wc, rr] = split(blt)

    def swap_part(panel, cols, n, first_half_rolled, part):
        (a0, a1), (b0, b1) = RUNS[part]
        a, b = panel[a0:a1, cols], panel[b0:b1, cols]
        rows = slice(part * 256, part * 256 + 256)
        if first_half_rolled:
            tms[n, rows] = jnp.where(left, roll64(a), b)
        else:
            tms[n, rows] = jnp.where(left, a, roll64(b))
        copy = remote(tms.at[n, rows], tmr.at[n, rows], TM + 2 * n + part, mate)
        copy.start()
        return copy

    def halo(low_src, low_dst, high_src, high_dst, n):
        down = remote(low_src, low_dst, DOWN + n, below)
        up = remote(high_src, high_dst, UP + n, above)

        @pl.when(has_below)
        def _():
            down.start()

        @pl.when(has_above)
        def _():
            up.start()

        return down, up

    def halo_arrived(copies):
        down, up = copies

        @pl.when(has_above)
        def _():
            down.wait_recv()

        @pl.when(has_below)
        def _():
            up.wait_recv()

    def halo_sent(copies):
        down, up = copies

        @pl.when(has_below)
        def _():
            down.wait_send()

        @pl.when(has_above)
        def _():
            up.wait_send()

    def scaled_part(panel, out, n, copy, part):
        copy.wait_recv()
        sign = jnp.where(t == 0, -1.0, 1.0)
        got = tmr[n, part * 256 : part * 256 + 256]
        for (b0, b1), from_mate in zip(RUNS[part], (got, roll64(got))):
            q0, q1 = b0 + 256, b1 + 256
            out[q0:q1, 0:128] = f[b0:b1, 0:128] * jnp.where(
                left, sign * from_mate, roll64(panel[b0:b1, 128:256])
            )
            out[q0:q1, 128:256] = f[b0:b1, 128:256] * panel[b0:b1, 0:128]

    def squares(panel):
        q = panel[...]
        q = jnp.sum((q * q).reshape(128, 8, 256), axis=0)
        q = q[:, 0:128] + q[:, 128:256]
        return q + roll64(q)

    def reduce_start(n):
        @pl.loop(0, team - 1)
        def _(i):
            pltpu.make_async_remote_copy(
                src_ref=redsrc.at[n], dst_ref=red.at[n, team - 2 - i],
                send_sem=redss.at[n], recv_sem=redrs.at[n],
                device_id=member(lax.rem(me + 1 + i, team)), device_id_type=MESH,
            ).start()

    def reduce_done(n):
        pltpu.make_async_copy(red.at[n], red.at[n], redrs.at[n]).wait()
        total = redsrc[n] + jnp.sum(red[n], axis=0)
        return (
            jnp.sum(total[0:8], axis=0, keepdims=True),
            jnp.sum(total[8:16], axis=0, keepdims=True),
        )

    def twice(v):
        return jnp.concatenate([v, v], axis=1)

    def forward_rows(i):
        win = pl.ds(pl.multiple_of(i * 256, 256), 768)
        rows = pl.ds(pl.multiple_of(i * 256, 256), 256)
        vhi = vh[win, :]
        acc = dot(kh[i], vhi) + dot(kl[i], vhi) + dot(kh[i], vl[win, :])
        im[rows, :] = d[rows, :] - acc

    def forward(value, copies):
        vh[256:1280, :], vl[256:1280, :] = split(value(256, 1280))

        @pl.loop(1, 3)
        def _(i):
            forward_rows(i)

        halo_arrived(copies)
        vh[0:256, :], vl[0:256, :] = split(value(0, 256))
        vh[1280:1536, :], vl[1280:1536, :] = split(value(1280, 1536))

        @pl.loop(0, 2)
        def _(i):
            forward_rows(i * 3)

    def back_part(i):
        zh, zl = split(im[pl.ds(pl.multiple_of(i * 256, 256), 256), :])
        return dot(kth[i], zh) + dot(ktl[i], zh) + dot(kth[i], zl)

    def backward(n, round_of):
        @pl.loop(0, 2)
        def _(i):
            y[pl.ds(pl.multiple_of(i * 768, 256), 768), :] = back_part(i * 3)

        copies = halo(
            y.at[0:256], yr.at[n, 1], y.at[1280:1536], yr.at[n, 0], 1 + 2 * n
        )

        redsrc[round_of, 8:16] = squares(im)
        reduce_start(round_of)

        @pl.loop(1, 3)
        def _(i):
            win = pl.ds(pl.multiple_of(i * 256, 256), 768)
            y[win, :] += back_part(i)

        return copies

    def scale_back(n, part):
        for side, (b0, b1) in enumerate(RUNS[part]):
            got = y[b0 + 256 : b1 + 256, :]
            if part == RIM:
                got = got + yr[n, side]
            y[b0 + 256 : b1 + 256, :] = f[b0:b1, :] * got
        return swap_part(y.at[256:1280], slice(0, 128), 1 + 2 * n, False, part)

    def apply_part(n, copy, source, out, alpha, part):
        copy.wait_recv()
        sign = jnp.where(t == 1, -1.0, 1.0)
        got = tmr[1 + 2 * n, part * 256 : part * 256 + 256]
        for (b0, b1), from_mate in zip(RUNS[part], (roll64(got), got)):
            g0, g1 = y[b0 + 256 : b1 + 256, 0:128], y[b0 + 256 : b1 + 256, 128:256]
            later = jnp.where(left, roll64(g0), sign * from_mate)
            out[b0:b1, 0:128] = source[b0:b1, 0:128] - alpha * (im[b0:b1, 0:128] - g1)
            out[b0:b1, 128:256] = source[b0:b1, 128:256] - alpha * (im[b0:b1, 128:256] - later)

    @pl.when(jnp.logical_not(has_below))
    def _():
        for ref in (sc1, sc2):
            ref[0:256, :] = jnp.zeros((256, 256), jnp.float32)
        for n in range(2):
            yr[n, 0] = jnp.zeros((256, 256), jnp.float32)

    @pl.when(jnp.logical_not(has_above))
    def _():
        for ref in (sc1, sc2):
            ref[1280:1536, :] = jnp.zeros((256, 256), jnp.float32)
        for n in range(2):
            yr[n, 1] = jnp.zeros((256, 256), jnp.float32)

    swapped = []
    last = slice(128, 256)
    make_field(h)
    kown.wait()
    make_bands(h)
    c_px[RIM].wait_recv()
    rim = swap_part(d, last, 0, True, RIM)
    c_small.wait_recv()
    make_field(o)
    c_kx.wait_recv()
    first_k = kraw.at[pl.ds(o * 12 + row * 3, 3)]
    c_ky = remote(first_k, first_k, KY, twin)
    c_ky.start()
    c_kc = remote(first_k, first_k, KC, mate)
    c_kc.start()
    scaled_part(d, sc1, 0, rim, RIM)
    h0 = halo(sc1.at[256:512], sc1.at[1280:1536], sc1.at[1024:1280], sc1.at[0:256], 0)
    c_px[INNER].wait_recv()
    inner = swap_part(d, last, 0, True, INNER)
    swapped += [rim, inner]
    redsrc[0, 0:8] = squares(d)
    c_ky.wait_recv()
    other_k = kraw.at[pl.ds(o * 12 + ((1 - g) * 2 + t) * 3, 3)]
    c_kd = remote(other_k, other_k, KD, mate)
    c_kd.start()
    scaled_part(d, sc1, 0, inner, INNER)
    c_kc.wait_recv()
    c_kd.wait_recv()
    make_bands(o)
    forward(lambda a, b: sc1[a:b, :], h0)
    b0 = backward(0, 0)
    inner = scale_back(0, INNER)
    rr0, im_sum = reduce_done(0)
    alpha1 = rr0 / im_sum
    alpha = alpha1
    apply_part(0, inner, d, r1, alpha, INNER)
    next_inner = swap_part(r1, last, 2, True, INNER)
    halo_arrived(b0)
    rim = scale_back(0, RIM)
    apply_part(0, rim, d, r1, alpha, RIM)
    next_rim = swap_part(r1, last, 2, True, RIM)
    swapped += [inner, rim, next_inner, next_rim]
    redsrc[1, 0:8] = squares(r1)
    redsrc[1, 8:16] = jnp.zeros((8, 128), jnp.float32)
    reduce_start(1)
    scaled_part(r1, sc2, 2, next_rim, RIM)
    h1 = halo(sc2.at[256:512], sc2.at[1280:1536], sc2.at[1024:1280], sc2.at[0:256], 2)
    c_r1 = remote(r1.at[peer_rows], r1p, R1X, peer)
    c_r1.start()
    scaled_part(r1, sc2, 2, next_inner, INNER)

    redsrc[2, 0:8] = jnp.zeros((8, 128), jnp.float32)
    rr1, _ = reduce_done(1)
    beta = rr1 / rr0
    beta2 = twice(beta)
    d[...] = r1[...] + beta2 * d[...]
    forward(lambda a, b: sc2[a:b, :] + beta2 * sc1[a:b, :], h1)
    halo_sent(b0)
    b1 = backward(1, 2)
    inner = scale_back(1, INNER)
    _, im_sum = reduce_done(2)
    alpha2 = rr1 / im_sum
    coef[0:8, :] = jnp.broadcast_to(alpha1 + alpha2 * beta, (8, 128))
    coef[8:16, :] = jnp.broadcast_to(alpha2, (8, 128))
    c_cx = remote(coef, coefp, CX, peer)
    c_cx.start()
    apply_part(1, inner, r1, r2, alpha2, INNER)
    c_r2 = [remote(r2.at[part_rows[n]], r2p.at[part_at[n]], R2X + n, peer) for n in range(2)]
    c_r2[INNER].start()
    halo_arrived(b1)
    rim = scale_back(1, RIM)
    apply_part(1, rim, r1, r2, alpha2, RIM)
    c_r2[RIM].start()
    swapped += [inner, rim]

    def unpack(own, other):
        low = jnp.where(is0, own, other)
        high = jnp.where(is0, other, own)
        return jnp.where(left, low, roll64(high)), jnp.where(left, roll64(low), high)

    c_cx.wait_recv()
    c_r1.wait_recv()
    low_coef = jnp.where(is0, coef[...], coefp[...])
    high_coef = jnp.where(is0, coefp[...], coef[...])
    full = jnp.where(left, low_coef, high_coef)
    cp, cr = full[0:1], full[8:9]

    @pl.loop(0, 4)
    def _(i):
        rows = pl.ds(pl.multiple_of(i * B, B), B)
        mine_rows = pl.ds(pl.multiple_of(h * 512 + i * B, B), B)
        for a in range(2):
            cols = slice(a * 128, a * 128 + 128)
            va, vb = unpack(r1[mine_rows, cols], r1p[rows, cols])
            sol_ref[a, rows, :] = cp * x_ref[a, rows, :] + cr * va
            sol_ref[a + 2, rows, :] = cp * x_ref[a + 2, rows, :] + cr * vb

    for part in (INNER, RIM):
        c_r2[part].wait_recv()
        for i in range(2):
            start = h * 256 if part == RIM else o * 256
            rows = pl.ds(pl.multiple_of(start + i * B, B), B)
            mine_rows = pl.ds(pl.multiple_of(h * 512 + start + i * B, B), B)
            for a in range(2):
                cols = slice(a * 128, a * 128 + 128)
                va, vb = unpack(r2[mine_rows, cols], r2p[rows, cols])
                res_ref[a, rows, :] = va
                res_ref[a + 2, rows, :] = vb

    for copy in [*c_px, c_small, c_kx, c_ky, c_kc, c_kd, *swapped, c_r1, c_cx, *c_r2]:
        copy.wait_send()
    for copies in (h0, h1, b1):
        halo_sent(copies)
    for n in range(3):
        pltpu.make_async_copy(red.at[n], red.at[n], redss.at[n]).wait()


def local(probes, phi, kcols, kblocks):
    pairs = lax.axis_size("space") // 2
    own = kcols.shape[0]
    f32, bf16 = jnp.float32, jnp.bfloat16
    vmem = pl.BlockSpec(memory_space=pltpu.VMEM)
    team = 2 * pairs
    return pl.pallas_call(
        functools.partial(kernel, pairs),
        out_shape=[jax.ShapeDtypeStruct(probes.shape, f32)] * 2,
        in_specs=[
            pl.BlockSpec(memory_space=pl.ANY), vmem,
            pl.BlockSpec(memory_space=pltpu.SMEM), pl.BlockSpec(memory_space=pl.ANY),
        ],
        out_specs=[vmem, vmem],
        scratch_shapes=[
            pltpu.VMEM((4, 512, 128), f32),
            pltpu.VMEM((512, 256), f32),
            pltpu.VMEM((1024, 256), f32),
            pltpu.VMEM((1024, 256), f32),
            pltpu.VMEM((1536, 256), f32),
            pltpu.VMEM((1536, 256), f32),
            pltpu.VMEM((1024, 256), f32),
            pltpu.VMEM((1536, 256), f32),
            pltpu.VMEM((1024, 256), f32),
            pltpu.VMEM((1024, 256), f32),
            pltpu.VMEM((512, 256), f32),
            pltpu.VMEM((512, 256), f32),
            pltpu.VMEM((2, 2, 256, 256), f32),
            pltpu.VMEM((4, 512, 128), f32),
            pltpu.VMEM((4, 512, 128), f32),
            pltpu.VMEM((2, 64, 128), f32),
            pltpu.VMEM((24, 128, 128), f32),
            pltpu.VMEM((4, 256, 768), bf16),
            pltpu.VMEM((4, 256, 768), bf16),
            pltpu.VMEM((4, 768, 256), bf16),
            pltpu.VMEM((4, 768, 256), bf16),
            pltpu.VMEM((1536, 256), bf16),
            pltpu.VMEM((1536, 256), bf16),
            pltpu.VMEM((3, 16, 128), f32),
            pltpu.VMEM((3, team - 1, 16, 128), f32),
            pltpu.VMEM((16, 128), f32),
            pltpu.VMEM((16, 128), f32),
            pltpu.SemaphoreType.DMA((NSEM,)),
            pltpu.SemaphoreType.DMA((NSEM,)),
            pltpu.SemaphoreType.DMA((3,)),
            pltpu.SemaphoreType.DMA((3,)),
            pltpu.SemaphoreType.DMA,
            pltpu.SemaphoreType.DMA,
        ],
        compiler_params=pltpu.CompilerParams(
            collective_id=0, has_side_effects=True, vmem_limit_bytes=60 * 1024 * 1024
        ),
    )(probes, phi, kcols, kblocks.reshape(own * 3, B, B))


def solution(mesh):
    panel = P(("groups", "tm"), "space", None)
    return jax.shard_map(
        local,
        mesh=mesh,
        in_specs=(
            panel, P(("groups", "tm"), "space"), P("space", None), P("space", None, None, None),
        ),
        out_specs=(panel, panel),
        check_vma=False,
    )
```

```python
import functools

import jax
import jax.numpy as jnp
from jax import lax
from jax.experimental import pallas as pl
from jax.experimental.pallas import tpu as pltpu
from jax.sharding import PartitionSpec as P

MESH = pl.DeviceIdType.MESH
B = 128
OFFS = (-2, -1, 1, 2)


SMALL, KX, KY, KC, KD, CX, PX, R1X, R2X, DOWN, UP, TM = 0, 1, 2, 3, 4, 5, 6, 8, 10, 12, 16, 20
NSEM = 28

RIM, INNER = 0, 1
RUNS = (((0, 256), (768, 1024)), ((256, 512), (512, 768)))


def roll64(x):
    return pltpu.roll(x, 64, axis=1)


def split(x):
    high = x.astype(jnp.bfloat16)
    return high, (x - high.astype(jnp.float32)).astype(jnp.bfloat16)


def dot(a, b):
    return jnp.dot(a, b, preferred_element_type=jnp.float32)


def kernel(
    pairs, x_hbm, phi_ref, cols_ref, k_ref, sol_ref, res_ref,
    x_ref, px, d, f, sc1, sc2, im, y, r1, r2, r1p, r2p, yr, tms, tmr, smalls, kraw,
    kh, kl, kth, ktl, vh, vl, redsrc, red, coef, coefp,
    ssem, rsem, redss, redrs, lsem, xsem,
):
    g, s, t = lax.axis_index("groups"), lax.axis_index("space"), lax.axis_index("tm")
    p, h = s // 2, s % 2
    o = 1 - h
    team = 2 * pairs
    me = p * 2 + t
    peer = (g, s + 1 - 2 * h, t)
    mate = (g, s, 1 - t)
    twin = (1 - g, s, t)
    below = (g, jnp.maximum(s - 2, 0), t)
    above = (g, jnp.minimum(s + 2, 2 * pairs - 1), t)
    has_below, has_above = p > 0, p < pairs - 1

    def member(index):
        return (g, (index // 2) * 2 + h, index % 2)

    barrier = pltpu.get_barrier_semaphore()

    @pl.loop(0, team - 1)
    def _(i):
        pl.semaphore_signal(
            barrier, inc=1, device_id=member(lax.rem(me + 1 + i, team)), device_id_type=MESH
        )

    pl.semaphore_signal(barrier, inc=1, device_id=peer, device_id_type=MESH)
    pl.semaphore_signal(barrier, inc=1, device_id=twin, device_id_type=MESH)
    xload = pltpu.make_async_copy(x_hbm, x_ref, xsem)
    xload.start()

    lane = lax.broadcasted_iota(jnp.int32, (1, 128), 1)
    left = lane < 64
    is0 = h == 0

    def remote(src, dst, index, device):
        return pltpu.make_async_remote_copy(
            src_ref=src, dst_ref=dst, send_sem=ssem.at[index], recv_sem=rsem.at[index],
            device_id=device, device_id_type=MESH,
        )

    part_rows = (
        pl.ds(pl.multiple_of(o * 768, 256), 256),
        pl.ds(pl.multiple_of(256 + o * 256, 256), 256),
    )
    part_at = (
        pl.ds(pl.multiple_of(o * 256, 256), 256),
        pl.ds(pl.multiple_of(h * 256, 256), 256),
    )
    own_part_rows = (
        pl.ds(pl.multiple_of(h * 768, 256), 256),
        pl.ds(pl.multiple_of(256 + h * 256, 256), 256),
    )
    own_part_at = (
        pl.ds(pl.multiple_of(h * 256, 256), 256),
        pl.ds(pl.multiple_of(o * 256, 256), 256),
    )
    kown = pltpu.make_async_copy(k_ref, kraw.at[pl.ds(h * 12, 12)], lsem)
    kown.start()

    sub = lax.broadcasted_iota(jnp.int32, (8, 128), 0)
    for j in range(4):
        chosen = jnp.zeros((8, 128), jnp.float32)
        for k in range(2):
            distance = cols_ref[j, 1 + k] - (s * 4 + j)
            for i1, off in enumerate(OFFS):
                hit = jnp.where(distance == off, 1.0, 0.0)
                chosen = jnp.where(sub == 4 * k + i1, hit, chosen)
        smalls[h, j * 16 : j * 16 + 8, :] = chosen
        part = phi_ref[:, j * B : j * B + B]
        smalls[h, j * 16 + 8 : j * 16 + 16, :] = jnp.concatenate([part, part], axis=0)

    xload.wait()

    @pl.loop(0, 4)
    def _(i):
        rows = pl.ds(pl.multiple_of(i * B, B), B)
        mine_rows = pl.ds(pl.multiple_of(h * 512 + i * B, B), B)
        for a in range(2):
            xa, xb = x_ref[a, rows, :], x_ref[a + 2, rows, :]
            low = jnp.where(left, xa, roll64(xb))
            high = jnp.where(left, roll64(xa), xb)
            cols = slice(a * 128, a * 128 + 128)
            px[rows, cols] = jnp.where(is0, high, low)
            d[mine_rows, cols] = jnp.where(is0, low, high)

    pl.semaphore_wait(barrier, team + 1)

    c_small = remote(smalls.at[h], smalls.at[h], SMALL, peer)
    c_small.start()
    c_px = [
        remote(px.at[own_part_at[n]], d.at[own_part_rows[n]], PX + n, peer) for n in range(2)
    ]
    c_px[RIM].start()
    row = g * 2 + t
    sent_k = pl.ds(h * 12 + row * 3, 3)
    c_kx = remote(k_ref.at[pl.ds(row * 3, 3)], kraw.at[sent_k], KX, peer)
    c_kx.start()
    c_px[INNER].start()

    def make_field(half):
        @pl.loop(0, 4)
        def _(j):
            e = jnp.exp(smalls[half, pl.ds(pl.multiple_of(j * 16 + 8, 8), 8), :])
            rows = pl.ds(pl.multiple_of(half * 512 + j * B, B), B)
            top = lax.broadcasted_iota(jnp.int32, (B, 128), 0) < 64
            for a in range(2):
                m = jnp.where(top, e[a : a + 1, :], e[a + 2 : a + 3, :])
                f[rows, a * 128 : a * 128 + 128] = m.T

    def make_bands(half):
        @pl.loop(0, 2)
        def _(jj):
            band = half * 2 + jj
            for ri in range(2):
                j = jj * 2 + ri
                k0, k1, k2 = (kraw[half * 12 + 3 * j + k] for k in range(3))
                t0, t1, t2 = k0.T, k1.T, k2.T
                sel = smalls[half, pl.ds(pl.multiple_of(j * 16, 8), 8), :]
                rr = slice(ri * B, ri * B + B)
                empty = 5 * (1 - ri)
                ec = slice(empty * B, empty * B + B)
                zero = jnp.zeros((B, B), jnp.bfloat16)
                kh[band, rr, ec] = zero
                kl[band, rr, ec] = zero
                kth[band, ec, rr] = zero
                ktl[band, ec, rr] = zero
                for off in range(-2, 3):
                    w = off + 2 + ri
                    wc = slice(w * B, w * B + B)
                    if off == 0:
                        blk, blt = k0, t0
                    else:
                        i1 = OFFS.index(off)
                        s1, s2 = sel[i1 : i1 + 1, :], sel[4 + i1 : 5 + i1, :]
                        blk, blt = s1 * k1 + s2 * k2, s1 * t1 + s2 * t2
                    kh[band, rr, wc], kl[band, rr, wc] = split(blk)
                    kth[band, wc, rr], ktl[band, wc, rr] = split(blt)

    def swap_part(panel, cols, n, first_half_rolled, part):
        (a0, a1), (b0, b1) = RUNS[part]
        a, b = panel[a0:a1, cols], panel[b0:b1, cols]
        rows = slice(part * 256, part * 256 + 256)
        if first_half_rolled:
            tms[n, rows] = jnp.where(left, roll64(a), b)
        else:
            tms[n, rows] = jnp.where(left, a, roll64(b))
        copy = remote(tms.at[n, rows], tmr.at[n, rows], TM + 2 * n + part, mate)
        copy.start()
        return copy

    def halo(low_src, low_dst, high_src, high_dst, n):
        down = remote(low_src, low_dst, DOWN + n, below)
        up = remote(high_src, high_dst, UP + n, above)

        @pl.when(has_below)
        def _():
            down.start()

        @pl.when(has_above)
        def _():
            up.start()

        return down, up

    def halo_arrived(copies):
        down, up = copies

        @pl.when(has_above)
        def _():
            down.wait_recv()

        @pl.when(has_below)
        def _():
            up.wait_recv()

    def halo_sent(copies):
        down, up = copies

        @pl.when(has_below)
        def _():
            down.wait_send()

        @pl.when(has_above)
        def _():
            up.wait_send()

    def scaled_part(panel, out, n, copy, part):
        copy.wait_recv()
        sign = jnp.where(t == 0, -1.0, 1.0)
        got = tmr[n, part * 256 : part * 256 + 256]
        for (b0, b1), from_mate in zip(RUNS[part], (got, roll64(got))):
            q0, q1 = b0 + 256, b1 + 256
            out[q0:q1, 0:128] = f[b0:b1, 0:128] * jnp.where(
                left, sign * from_mate, roll64(panel[b0:b1, 128:256])
            )
            out[q0:q1, 128:256] = f[b0:b1, 128:256] * panel[b0:b1, 0:128]

    def squares(panel):
        q = panel[...]
        q = jnp.sum((q * q).reshape(128, 8, 256), axis=0)
        q = q[:, 0:128] + q[:, 128:256]
        return q + roll64(q)

    def reduce_start(n):
        @pl.loop(0, team - 1)
        def _(i):
            pltpu.make_async_remote_copy(
                src_ref=redsrc.at[n], dst_ref=red.at[n, team - 2 - i],
                send_sem=redss.at[n], recv_sem=redrs.at[n],
                device_id=member(lax.rem(me + 1 + i, team)), device_id_type=MESH,
            ).start()

    def reduce_done(n):
        pltpu.make_async_copy(red.at[n], red.at[n], redrs.at[n]).wait()
        total = redsrc[n] + jnp.sum(red[n], axis=0)
        return (
            jnp.sum(total[0:8], axis=0, keepdims=True),
            jnp.sum(total[8:16], axis=0, keepdims=True),
        )

    def twice(v):
        return jnp.concatenate([v, v], axis=1)

    def forward_rows(i):
        win = pl.ds(pl.multiple_of(i * 256, 256), 768)
        rows = pl.ds(pl.multiple_of(i * 256, 256), 256)
        vhi = vh[win, :]
        acc = dot(kh[i], vhi) + dot(kl[i], vhi) + dot(kh[i], vl[win, :])
        im[rows, :] = d[rows, :] - acc

    def forward(value, copies):
        vh[256:1280, :], vl[256:1280, :] = split(value(256, 1280))

        @pl.loop(1, 3)
        def _(i):
            forward_rows(i)

        halo_arrived(copies)
        vh[0:256, :], vl[0:256, :] = split(value(0, 256))
        vh[1280:1536, :], vl[1280:1536, :] = split(value(1280, 1536))

        @pl.loop(0, 2)
        def _(i):
            forward_rows(i * 3)

    def back_part(i):
        zh, zl = split(im[pl.ds(pl.multiple_of(i * 256, 256), 256), :])
        return dot(kth[i], zh) + dot(ktl[i], zh) + dot(kth[i], zl)

    def backward(n, round_of):
        @pl.loop(0, 2)
        def _(i):
            y[pl.ds(pl.multiple_of(i * 768, 256), 768), :] = back_part(i * 3)

        copies = halo(
            y.at[0:256], yr.at[n, 1], y.at[1280:1536], yr.at[n, 0], 1 + 2 * n
        )

        redsrc[round_of, 8:16] = squares(im)
        reduce_start(round_of)

        @pl.loop(1, 3)
        def _(i):
            win = pl.ds(pl.multiple_of(i * 256, 256), 768)
            y[win, :] += back_part(i)

        return copies

    def scale_back(n, part):
        for side, (b0, b1) in enumerate(RUNS[part]):
            got = y[b0 + 256 : b1 + 256, :]
            if part == RIM:
                got = got + yr[n, side]
            y[b0 + 256 : b1 + 256, :] = f[b0:b1, :] * got
        return swap_part(y.at[256:1280], slice(0, 128), 1 + 2 * n, False, part)

    def apply_part(n, copy, source, out, alpha, part):
        copy.wait_recv()
        sign = jnp.where(t == 1, -1.0, 1.0)
        got = tmr[1 + 2 * n, part * 256 : part * 256 + 256]
        for (b0, b1), from_mate in zip(RUNS[part], (roll64(got), got)):
            g0, g1 = y[b0 + 256 : b1 + 256, 0:128], y[b0 + 256 : b1 + 256, 128:256]
            later = jnp.where(left, roll64(g0), sign * from_mate)
            out[b0:b1, 0:128] = source[b0:b1, 0:128] - alpha * (im[b0:b1, 0:128] - g1)
            out[b0:b1, 128:256] = source[b0:b1, 128:256] - alpha * (im[b0:b1, 128:256] - later)

    @pl.when(jnp.logical_not(has_below))
    def _():
        for ref in (sc1, sc2):
            ref[0:256, :] = jnp.zeros((256, 256), jnp.float32)
        for n in range(2):
            yr[n, 0] = jnp.zeros((256, 256), jnp.float32)

    @pl.when(jnp.logical_not(has_above))
    def _():
        for ref in (sc1, sc2):
            ref[1280:1536, :] = jnp.zeros((256, 256), jnp.float32)
        for n in range(2):
            yr[n, 1] = jnp.zeros((256, 256), jnp.float32)

    swapped = []
    last = slice(128, 256)
    make_field(h)
    kown.wait()
    make_bands(h)
    c_px[RIM].wait_recv()
    rim = swap_part(d, last, 0, True, RIM)
    c_small.wait_recv()
    make_field(o)
    c_kx.wait_recv()
    first_k = kraw.at[pl.ds(o * 12 + row * 3, 3)]
    c_ky = remote(first_k, first_k, KY, twin)
    c_ky.start()
    c_kc = remote(first_k, first_k, KC, mate)
    c_kc.start()
    scaled_part(d, sc1, 0, rim, RIM)
    h0 = halo(sc1.at[256:512], sc1.at[1280:1536], sc1.at[1024:1280], sc1.at[0:256], 0)
    c_px[INNER].wait_recv()
    inner = swap_part(d, last, 0, True, INNER)
    swapped += [rim, inner]
    redsrc[0, 0:8] = squares(d)
    c_ky.wait_recv()
    other_k = kraw.at[pl.ds(o * 12 + ((1 - g) * 2 + t) * 3, 3)]
    c_kd = remote(other_k, other_k, KD, mate)
    c_kd.start()
    scaled_part(d, sc1, 0, inner, INNER)
    c_kc.wait_recv()
    c_kd.wait_recv()
    make_bands(o)
    forward(lambda a, b: sc1[a:b, :], h0)
    b0 = backward(0, 0)
    inner = scale_back(0, INNER)
    rr0, im_sum = reduce_done(0)
    alpha1 = rr0 / im_sum
    alpha = alpha1
    apply_part(0, inner, d, r1, alpha, INNER)
    next_inner = swap_part(r1, last, 2, True, INNER)
    c_r1 = [remote(r1.at[part_rows[n]], r1p.at[part_at[n]], R1X + n, peer) for n in range(2)]
    c_r1[INNER].start()
    halo_arrived(b0)
    rim = scale_back(0, RIM)
    apply_part(0, rim, d, r1, alpha, RIM)
    next_rim = swap_part(r1, last, 2, True, RIM)
    c_r1[RIM].start()
    swapped += [inner, rim, next_inner, next_rim]
    redsrc[1, 0:8] = squares(r1)
    redsrc[1, 8:16] = jnp.zeros((8, 128), jnp.float32)
    reduce_start(1)
    scaled_part(r1, sc2, 2, next_rim, RIM)
    h1 = halo(sc2.at[256:512], sc2.at[1280:1536], sc2.at[1024:1280], sc2.at[0:256], 2)
    scaled_part(r1, sc2, 2, next_inner, INNER)

    redsrc[2, 0:8] = jnp.zeros((8, 128), jnp.float32)
    rr1, _ = reduce_done(1)
    beta = rr1 / rr0
    beta2 = twice(beta)
    d[...] = r1[...] + beta2 * d[...]
    forward(lambda a, b: sc2[a:b, :] + beta2 * sc1[a:b, :], h1)
    halo_sent(b0)
    b1 = backward(1, 2)
    inner = scale_back(1, INNER)
    _, im_sum = reduce_done(2)
    alpha2 = rr1 / im_sum
    coef[0:8, :] = jnp.broadcast_to(alpha1 + alpha2 * beta, (8, 128))
    coef[8:16, :] = jnp.broadcast_to(alpha2, (8, 128))
    c_cx = remote(coef, coefp, CX, peer)
    c_cx.start()
    apply_part(1, inner, r1, r2, alpha2, INNER)
    c_r2 = [remote(r2.at[part_rows[n]], r2p.at[part_at[n]], R2X + n, peer) for n in range(2)]
    c_r2[INNER].start()
    halo_arrived(b1)
    rim = scale_back(1, RIM)
    apply_part(1, rim, r1, r2, alpha2, RIM)
    c_r2[RIM].start()
    swapped += [inner, rim]

    def unpack(own, other):
        low = jnp.where(is0, own, other)
        high = jnp.where(is0, other, own)
        return jnp.where(left, low, roll64(high)), jnp.where(left, roll64(low), high)

    c_cx.wait_recv()
    c_r1[INNER].wait_recv()
    c_r1[RIM].wait_recv()
    low_coef = jnp.where(is0, coef[...], coefp[...])
    high_coef = jnp.where(is0, coefp[...], coef[...])
    full = jnp.where(left, low_coef, high_coef)
    cp, cr = full[0:1], full[8:9]

    @pl.loop(0, 4)
    def _(i):
        rows = pl.ds(pl.multiple_of(i * B, B), B)
        mine_rows = pl.ds(pl.multiple_of(h * 512 + i * B, B), B)
        for a in range(2):
            cols = slice(a * 128, a * 128 + 128)
            va, vb = unpack(r1[mine_rows, cols], r1p[rows, cols])
            sol_ref[a, rows, :] = cp * x_ref[a, rows, :] + cr * va
            sol_ref[a + 2, rows, :] = cp * x_ref[a + 2, rows, :] + cr * vb

    for part in (INNER, RIM):
        c_r2[part].wait_recv()
        for i in range(2):
            start = h * 256 if part == RIM else o * 256
            rows = pl.ds(pl.multiple_of(start + i * B, B), B)
            mine_rows = pl.ds(pl.multiple_of(h * 512 + start + i * B, B), B)
            for a in range(2):
                cols = slice(a * 128, a * 128 + 128)
                va, vb = unpack(r2[mine_rows, cols], r2p[rows, cols])
                res_ref[a, rows, :] = va
                res_ref[a + 2, rows, :] = vb

    for copy in [*c_px, c_small, c_kx, c_ky, c_kc, c_kd, *swapped, *c_r1, c_cx, *c_r2]:
        copy.wait_send()
    for copies in (h0, h1, b1):
        halo_sent(copies)
    for n in range(3):
        pltpu.make_async_copy(red.at[n], red.at[n], redss.at[n]).wait()


def local(probes, phi, kcols, kblocks):
    pairs = lax.axis_size("space") // 2
    own = kcols.shape[0]
    f32, bf16 = jnp.float32, jnp.bfloat16
    vmem = pl.BlockSpec(memory_space=pltpu.VMEM)
    team = 2 * pairs
    return pl.pallas_call(
        functools.partial(kernel, pairs),
        out_shape=[jax.ShapeDtypeStruct(probes.shape, f32)] * 2,
        in_specs=[
            pl.BlockSpec(memory_space=pl.ANY), vmem,
            pl.BlockSpec(memory_space=pltpu.SMEM), pl.BlockSpec(memory_space=pl.ANY),
        ],
        out_specs=[vmem, vmem],
        scratch_shapes=[
            pltpu.VMEM((4, 512, 128), f32),
            pltpu.VMEM((512, 256), f32),
            pltpu.VMEM((1024, 256), f32),
            pltpu.VMEM((1024, 256), f32),
            pltpu.VMEM((1536, 256), f32),
            pltpu.VMEM((1536, 256), f32),
            pltpu.VMEM((1024, 256), f32),
            pltpu.VMEM((1536, 256), f32),
            pltpu.VMEM((1024, 256), f32),
            pltpu.VMEM((1024, 256), f32),
            pltpu.VMEM((512, 256), f32),
            pltpu.VMEM((512, 256), f32),
            pltpu.VMEM((2, 2, 256, 256), f32),
            pltpu.VMEM((4, 512, 128), f32),
            pltpu.VMEM((4, 512, 128), f32),
            pltpu.VMEM((2, 64, 128), f32),
            pltpu.VMEM((24, 128, 128), f32),
            pltpu.VMEM((4, 256, 768), bf16),
            pltpu.VMEM((4, 256, 768), bf16),
            pltpu.VMEM((4, 768, 256), bf16),
            pltpu.VMEM((4, 768, 256), bf16),
            pltpu.VMEM((1536, 256), bf16),
            pltpu.VMEM((1536, 256), bf16),
            pltpu.VMEM((3, 16, 128), f32),
            pltpu.VMEM((3, team - 1, 16, 128), f32),
            pltpu.VMEM((16, 128), f32),
            pltpu.VMEM((16, 128), f32),
            pltpu.SemaphoreType.DMA((NSEM,)),
            pltpu.SemaphoreType.DMA((NSEM,)),
            pltpu.SemaphoreType.DMA((3,)),
            pltpu.SemaphoreType.DMA((3,)),
            pltpu.SemaphoreType.DMA,
            pltpu.SemaphoreType.DMA,
        ],
        compiler_params=pltpu.CompilerParams(
            collective_id=0, has_side_effects=True, vmem_limit_bytes=54 * 1024 * 1024
        ),
    )(probes, phi, kcols, kblocks.reshape(own * 3, B, B))


def solution(mesh):
    panel = P(("groups", "tm"), "space", None)
    return jax.shard_map(
        local,
        mesh=mesh,
        in_specs=(
            panel, P(("groups", "tm"), "space"), P("space", None), P("space", None, None, None),
        ),
        out_specs=(panel, panel),
        check_vma=False,
    )
```
